32 devices in a mesh: grp: 8 (over z, y), blk: 4 (over x, core).
Axes of the slice: x: 2, y: 2, z: 4, core: 2. Of those that a mesh axis runs over, the one named last changes fastest.
Arguments:
- src_codes: int32 [32768, 1024], P(('grp', 'blk')), may hold values from -119 to 119
- src_exps: int32 [32768, 8], P(('grp', 'blk')), may hold values from 0 to 3
- signs: int32 [32768, 256], P(('grp', 'blk')), may hold values from 0 to 1
- tgt_codes: int32 [1024, 1024], P('blk'), may hold values from -119 to 119
- tgt_exps: int32 [1024, 8], P('blk'), may hold values from 0 to 3
Outputs:
- kernel_product: float32 [1024, 256], P('blk', 'grp')
The draws below stay inside these ranges and needn't reach their ends.
All inputs are finite; a program needn't handle non-finite values.
Results may differ from the reference program's by a relative error of at most 0.003.
Values may be sent and summed in bfloat16 or wider, within the bound.
A program may use at most 64 MiB of HBM per device.

```python
import math
import jax
import jax.numpy as jnp
from jax import lax

D = 1024
QBLOCK = 128
RHS = 256
S_DEV = 1024
TARGETS = 1024
SOURCES = 32768


latent_width = 16


center_reach = 5


nudge_reach = 3


anchor_reach = 28


jitter_reach = 3


code_limit = 119


block_scale = 4


group_rows = 128


def group_tables(key):
    groups = max(SOURCES // group_rows, 1)
    centers = jax.random.randint(jax.random.fold_in(key, 201), (groups, latent_width), -center_reach, center_reach + 1, dtype=jnp.int32)
    anchors = jax.random.randint(jax.random.fold_in(key, 205), (groups, D), -anchor_reach, anchor_reach + 1, dtype=jnp.int32)
    basis = jax.random.randint(jax.random.fold_in(key, 202), (latent_width, D), 0, 2, dtype=jnp.int32) * 2 - 1
    return (groups, centers, anchors, basis)


def quantize_rows(combined, level):
    count = combined.shape[0]
    blocks = D // QBLOCK
    valued = (combined * block_scale).reshape(count, blocks, QBLOCK)
    largest = jnp.max(jnp.abs(valued), axis=2)
    needed = (largest > code_limit).astype(jnp.int32) + (largest > 2 * code_limit).astype(jnp.int32) + (largest > 4 * code_limit).astype(jnp.int32)
    lowered = (level == 0).astype(jnp.int32)
    raised = (level == 3).astype(jnp.int32)
    exponent = jnp.clip(needed - lowered + raised, 0, 3)
    divisor = 1 + (exponent >= 1).astype(jnp.int32) + 2 * (exponent >= 2).astype(jnp.int32) + 4 * (exponent >= 3).astype(jnp.int32)
    code_rows = jnp.clip(jnp.floor_divide(valued, divisor[:, :, None]), -code_limit, code_limit)
    return (code_rows.reshape(count, D), exponent)


def build_points(key, count, salt):
    groups, centers, anchors, basis = group_tables(key)
    chosen = jax.random.randint(jax.random.fold_in(key, salt), (count,), 0, groups, dtype=jnp.int32)
    nudge = jax.random.randint(jax.random.fold_in(key, salt + 1), (count, latent_width), -nudge_reach, nudge_reach + 1, dtype=jnp.int32)
    jitter = jax.random.randint(jax.random.fold_in(key, salt + 2), (count, D), -jitter_reach, jitter_reach + 1, dtype=jnp.int32)
    level = jax.random.randint(jax.random.fold_in(key, salt + 3), (count, D // QBLOCK), 0, 4, dtype=jnp.int32)
    latent = jnp.take(centers, chosen, axis=0) + nudge
    combined = jnp.dot(latent, basis, preferred_element_type=jnp.int32) + jnp.take(anchors, chosen, axis=0) + jitter
    return quantize_rows(combined, level)


def draw_src_codes(key, part):
    return build_points(key, SOURCES, 210)[0]


def draw_src_exps(key, part):
    return build_points(key, SOURCES, 210)[1]


def draw_tgt_codes(key, part):
    return build_points(key, TARGETS, 220)[0]


def draw_tgt_exps(key, part):
    return build_points(key, TARGETS, 220)[1]


def with_ends(values, rng, low, high):
    longest = values.shape.index(max(values.shape))
    spots = []
    for shift in (0, 1):
        where = [jax.random.randint(jax.random.fold_in(rng, axis), (), 0, length) for axis, length in enumerate(values.shape)]
        where[longest] = (where[longest] + shift) % values.shape[longest]
        spots.append(tuple(where))
    return values.at[spots[0]].set(low).at[spots[1]].set(high)


def setup_inputs(seed: int = 0) -> dict:
    key_of = jax.random.split(jax.random.key(seed), 6)
    return {
        "src_codes": draw_src_codes(jax.random.fold_in(key_of[5], 71), 0),
        "src_exps": draw_src_exps(jax.random.fold_in(key_of[5], 71), 0),
        "signs": with_ends(jax.random.randint(key_of[2], (SOURCES, RHS), 0, 2), jax.random.fold_in(key_of[2], 1), 0, 1).astype(jnp.int32),
        "tgt_codes": draw_tgt_codes(jax.random.fold_in(key_of[5], 71), 0),
        "tgt_exps": draw_tgt_exps(jax.random.fold_in(key_of[5], 71), 0),
    }


kernel_rate = 20.0

def dequantize(codes, exponents):
    points, columns = codes.shape
    blocks = exponents.shape[1]
    factor = jnp.zeros(exponents.shape, jnp.float32)
    for level_index in range(4):
        factor = factor + jnp.where(exponents == level_index, 2.0 ** (level_index - 9), 0.0)
    scaled_codes = codes.reshape(points, blocks, columns // blocks).astype(jnp.float32) * factor[:, :, None]
    return scaled_codes.reshape(points, columns).astype(jnp.bfloat16)

def squares(points_bf):
    widened = points_bf.astype(jnp.float32)
    return lax.optimization_barrier(jnp.sum(widened * widened, axis=1))

def kernel_block(targets_bf, sources_bf, source_sq, rhs_values):
    target_sq = squares(targets_bf)
    inner_products = lax.dot_general(targets_bf, sources_bf, (((1,), (1,)), ((), ())), preferred_element_type=jnp.float32)
    squared = target_sq[:, None] + source_sq[None, :] - 2.0 * inner_products
    scaled = kernel_rate * jnp.sqrt(squared) / math.sqrt(targets_bf.shape[1])
    matern = ((1.0 + scaled + scaled * scaled / 3.0) * jnp.exp(-scaled)).astype(jnp.bfloat16)
    return jnp.dot(matern, rhs_values, preferred_element_type=jnp.float32)

def reference(src_codes, src_exps, signs, tgt_codes, tgt_exps):
    sources_bf = dequantize(src_codes, src_exps)
    targets_bf = dequantize(tgt_codes, tgt_exps)
    rhs_values = (2 * signs - 1).astype(jnp.bfloat16)
    source_sq = squares(sources_bf)
    groups = SOURCES // S_DEV
    stacked = (sources_bf.reshape(groups, S_DEV, D), source_sq.reshape(groups, S_DEV), rhs_values.reshape(groups, S_DEV, RHS))

    def advance(running, sliced):
        return (running + kernel_block(targets_bf, sliced[0], sliced[1], sliced[2]), None)
    running, _ = lax.scan(advance, jnp.zeros((TARGETS, RHS), jnp.float32), stacked)
    return running * (4.0 / math.sqrt(SOURCES))
```

```python
import functools
import math

import jax
import jax.numpy as jnp
from jax import lax
from jax.experimental import pallas as pl
from jax.experimental.pallas import tpu as pltpu
from jax.sharding import PartitionSpec as P

kernel_rate = 20.0
lanes = 128
src_chunks = 4
hop_chunks = 4
slab = 256
smallest = 2.0**-40
MESH = pl.DeviceIdType.MESH


def row_slice(start, size):
    return pl.ds(pl.multiple_of(start, size), size)


def dequantize_rows(codes, exps, start, count, gain, dst):
    levels = exps[:, row_slice(start, count)]
    factor = jnp.where(
        levels == 0,
        gain * 2.0**-9,
        jnp.where(levels == 1, gain * 2.0**-8, jnp.where(levels == 2, gain * 2.0**-7, gain * 2.0**-6)),
    ).astype(jnp.float32)
    factor = jnp.transpose(factor)
    blocks = exps.shape[0]
    width = codes.shape[1] // blocks
    total = None
    for j in range(blocks):
        columns = slice(j * width, (j + 1) * width)
        points = codes[row_slice(start, count), columns].astype(jnp.float32) * factor[:, j : j + 1]
        dst[row_slice(start, count), columns] = points.astype(jnp.bfloat16)
        total = points * points if total is None else total + points * points
    return total


def square_rows(points_ref, start, count):
    total = None
    for j in range(points_ref.shape[1] // lanes):
        points = points_ref[row_slice(start, count), j * lanes : (j + 1) * lanes].astype(jnp.float32)
        total = points * points if total is None else total + points * points
    return total


def kernel(
    ng, nb, sc_hbm, se_hbm, sg_hbm, tc_hbm, te_hbm, out_ref,
    sc, se, sg, tc, te, src, ssq, tgt, tsq, rhs, mat, acc,
    plane_send, plane_recv, hop_send, hop_recv, total,
    load_sem, core_send_sem, core_recv_sem, x_send_sem, x_recv_sem, f_send_sem, f_recv_sem,
    p_send_sem, p_recv_sem, h_send_sem, h_recv_sem,
):
    g = lax.axis_index("grp")
    b = lax.axis_index("blk")
    hs = nb // 2
    h, c = b // 2, lax.rem(b, 2)
    rows, width = sc.shape
    trows = tc.shape[0]
    rhs_count = sg.shape[1]
    part = rhs_count // ng
    half = trows // 2
    chunk = half // hop_chunks
    src_chunk = rows // src_chunks

    partner = (g, b + 1 - 2 * c)
    peers = [(g, lax.rem(h + j, hs) * 2 + c) for j in range(1, hs)]
    owners = [(g, lax.rem(h - j + hs, hs) * 2 + c) for j in range(1, hs)]
    plane = [(lax.rem(g + i, ng), b) for i in range(1, ng)]
    low, high = lax.rem(g, 2), lax.rem(g // 2, 2)
    side = lax.rem(low + high, 2)
    forward_to = [(g + 1 - 2 * low, b), (g + 2 - 4 * high, b)]

    load_te = pltpu.make_async_copy(te_hbm, te, load_sem.at[0])
    load_te.start()
    load_tc = pltpu.make_async_copy(tc_hbm, tc, load_sem.at[1])
    load_tc.start()
    load_se = pltpu.make_async_copy(se_hbm, se, load_sem.at[2])
    load_se.start()
    load_sc = []
    for k in range(src_chunks):
        piece = pl.ds(k * src_chunk, src_chunk)
        load_sc.append(pltpu.make_async_copy(sc_hbm.at[piece], sc.at[piece], load_sem.at[4 + k]))
        load_sc[-1].start()
    load_sg = pltpu.make_async_copy(sg_hbm, sg, load_sem.at[3])
    load_sg.start()

    barrier = pltpu.get_barrier_semaphore()
    greeted = [partner] + peers + plane
    for device in greeted:
        pl.semaphore_signal(barrier, inc=1, device_id=device, device_id_type=MESH)

    def own_targets(part_index):
        start = part_index * half
        squares = dequantize_rows(tc, te, start, half, -2.0, tgt.at[0])
        tsq[0, pl.ds(part_index, 1), :] = 0.25 * jnp.sum(jnp.transpose(squares), axis=0, keepdims=True)

    load_te.wait()
    load_tc.wait()
    own_targets(side)
    pl.semaphore_wait(barrier, len(greeted))

    def hop_rows(which, q):
        return row_slice(which * half + q * chunk, chunk)

    def x_copy(j, q):
        piece = hop_rows(side, q)
        return pltpu.make_async_remote_copy(
            src_ref=tgt.at[0, piece], dst_ref=tgt.at[j, piece],
            send_sem=x_send_sem.at[j - 1, q], recv_sem=x_recv_sem.at[j - 1, q],
            device_id=peers[j - 1], device_id_type=MESH,
        )

    def f_copy(j, q, which):
        piece = hop_rows(which, q)
        return pltpu.make_async_remote_copy(
            src_ref=tgt.at[j, piece], dst_ref=tgt.at[j, piece],
            send_sem=f_send_sem.at[j - 1, q], recv_sem=f_recv_sem.at[j - 1, q],
            device_id=forward_to[q % 2], device_id_type=MESH,
        )

    for q in range(hop_chunks):
        for j in range(1, hs):
            x_copy(j, q).start()
    own_targets(1 - side)

    def forward(q):
        for j in range(1, hs):
            x_copy(j, q).wait_recv()
            f_copy(j, q, side).start()

    def src_copy(k):
        return pltpu.make_async_remote_copy(
            src_ref=src.at[0, pl.ds(k * src_chunk, src_chunk)],
            dst_ref=src.at[1, pl.ds(k * src_chunk, src_chunk)],
            send_sem=core_send_sem.at[k], recv_sem=core_recv_sem.at[k],
            device_id=partner, device_id_type=MESH,
        )

    rhs_copy = pltpu.make_async_remote_copy(
        src_ref=rhs.at[0], dst_ref=rhs.at[1],
        send_sem=core_send_sem.at[src_chunks], recv_sem=core_recv_sem.at[src_chunks],
        device_id=partner, device_id_type=MESH,
    )

    def keep_source_squares(slot, start, squares):
        summed = jnp.sum(squares, axis=1, keepdims=True)
        ssq[slot, row_slice(start, lanes), :] = jnp.broadcast_to(summed, (lanes, lanes))

    load_se.wait()
    for k in range(src_chunks):
        load_sc[k].wait()

        @pl.loop(0, src_chunk // lanes)
        def _(i):
            start = k * src_chunk + i * lanes
            keep_source_squares(0, start, dequantize_rows(sc, se, start, lanes, 1.0, src.at[0]))

        src_copy(k).start()

    load_sg.wait()

    @pl.loop(0, rows // lanes)
    def _(i):
        signs = sg[row_slice(i * lanes, lanes), :].astype(jnp.float32)
        values = jnp.transpose(2.0 * signs - 1.0)
        rhs[0, :, row_slice(i * lanes, lanes)] = values.astype(jnp.bfloat16)

    rhs_copy.start()
    forward(0)

    rate = kernel_rate / math.sqrt(width)

    def matern_slabs(slot, j):
        target_sq = jnp.concatenate([tsq[j, 0:1, :], tsq[j, 1:2, :]], axis=1)

        @pl.loop(0, rows // slab)
        def _(i):
            piece = row_slice(i * slab, slab)
            inner = lax.dot_general(
                src[slot, piece, :], tgt[j], (((1,), (1,)), ((), ())),
                preferred_element_type=jnp.float32,
            )
            source_sq = ssq[slot, piece, :]
            source_sq = jnp.concatenate([source_sq] * (trows // lanes), axis=1)
            squared = jnp.maximum((source_sq + target_sq) + inner, smallest)
            distance = squared * lax.rsqrt(squared)
            decay = jnp.exp2(distance * (-rate * math.log2(math.e)))
            growth = 1.0 + distance * (rate + distance * (rate * rate / 3.0))
            mat[slot, piece, :] = (growth * decay).astype(jnp.bfloat16)

    def plane_copies(j):
        copies = []
        for i in range(1, ng):
            copies.append(pltpu.make_async_remote_copy(
                src_ref=plane_send.at[j, row_slice(plane[i - 1][0] * part, part)],
                dst_ref=plane_recv.at[j, i - 1],
                send_sem=p_send_sem.at[j], recv_sem=p_recv_sem.at[j],
                device_id=plane[i - 1], device_id_type=MESH,
            ))
        return copies

    def multiply_and_send(j):
        sums = jnp.dot(rhs[0], mat[0], preferred_element_type=jnp.float32)
        sums = sums + jnp.dot(rhs[1], mat[1], preferred_element_type=jnp.float32)
        acc[...] = sums
        plane_send[j] = sums.astype(jnp.bfloat16)
        for copy in plane_copies(j):
            copy.start()
        total[j] = acc[row_slice(g * part, part), :]

    def plane_total(j):
        pltpu.make_async_copy(plane_recv.at[j], plane_recv.at[j], p_recv_sem.at[j]).wait()
        sums = total[j]
        for i in range(ng - 1):
            sums = sums + plane_recv[j, i].astype(jnp.float32)
        return sums

    matern_slabs(0, 0)
    forward(1)
    for k in range(src_chunks):
        src_copy(k).wait_recv()

    @pl.loop(0, rows // lanes)
    def _(i):
        keep_source_squares(1, i * lanes, square_rows(src.at[1], i * lanes, lanes))

    matern_slabs(1, 0)
    forward(2)
    rhs_copy.wait_recv()
    multiply_and_send(0)
    for q in range(3, hop_chunks):
        forward(q)

    def hop_copy(j):
        return pltpu.make_async_remote_copy(
            src_ref=hop_send.at[j - 1], dst_ref=hop_recv.at[j - 1],
            send_sem=h_send_sem.at[j - 1], recv_sem=h_recv_sem.at[j - 1],
            device_id=owners[j - 1], device_id_type=MESH,
        )

    def target_squares(j, which):
        squares = square_rows(tgt.at[j], which * half, half)
        tsq[j, pl.ds(which, 1), :] = 0.25 * jnp.sum(jnp.transpose(squares), axis=0, keepdims=True)

    for j in range(1, hs):
        target_squares(j, side)
        for q in range(hop_chunks):
            f_copy(j, q, 1 - side).wait_recv()
        target_squares(j, 1 - side)
        matern_slabs(0, j)
        matern_slabs(1, j)
        multiply_and_send(j)

    result = plane_total(0)
    for j in range(1, hs):
        hop_send[j - 1] = plane_total(j)
        hop_copy(j).start()
    for j in range(1, hs):
        hop_copy(j).wait_recv()
        result = result + hop_recv[j - 1]
    out_ref[...] = result * (4.0 / math.sqrt(rows * ng * nb))

    for j in range(1, hs):
        for q in range(hop_chunks):
            x_copy(j, q).wait_send()
            f_copy(j, q, side).wait_send()
        hop_copy(j).wait_send()
    for k in range(src_chunks):
        src_copy(k).wait_send()
    rhs_copy.wait_send()
    for j in range(hs):
        pltpu.make_async_copy(plane_recv.at[j], plane_recv.at[j], p_send_sem.at[j]).wait()


def per_device(src_codes, src_exps, signs, tgt_codes, tgt_exps):
    ng, nb = lax.axis_size("grp"), lax.axis_size("blk")
    hs = nb // 2
    rows, width = src_codes.shape
    trows = tgt_codes.shape[0]
    rhs_count = signs.shape[1]
    blocks = src_exps.shape[1]
    part = rhs_count // ng
    f32, bf16, i32 = jnp.float32, jnp.bfloat16, jnp.int32
    dma = pltpu.SemaphoreType.DMA
    out = pl.pallas_call(
        functools.partial(kernel, ng, nb),
        out_shape=jax.ShapeDtypeStruct((part, trows), f32),
        in_specs=[pl.BlockSpec(memory_space=pl.ANY)] * 5,
        out_specs=pl.BlockSpec(memory_space=pltpu.VMEM),
        scratch_shapes=[
            pltpu.VMEM((rows, width), i32),
            pltpu.VMEM((blocks, rows), i32),
            pltpu.VMEM((rows, rhs_count), i32),
            pltpu.VMEM((trows, width), i32),
            pltpu.VMEM((blocks, trows), i32),
            pltpu.VMEM((2, rows, width), bf16),
            pltpu.VMEM((2, rows, lanes), f32),
            pltpu.VMEM((hs, trows, width), bf16),
            pltpu.VMEM((hs, 2, trows // 2), f32),
            pltpu.VMEM((2, rhs_count, rows), bf16),
            pltpu.VMEM((2, rows, trows), bf16),
            pltpu.VMEM((rhs_count, trows), f32),
            pltpu.VMEM((hs, rhs_count, trows), bf16),
            pltpu.VMEM((hs, ng - 1, part, trows), bf16),
            pltpu.VMEM((hs - 1, part, trows), f32),
            pltpu.VMEM((hs - 1, part, trows), f32),
            pltpu.VMEM((hs, part, trows), f32),
            dma((4 + src_chunks,)),
            dma((src_chunks + 1,)),
            dma((src_chunks + 1,)),
            dma((hs - 1, hop_chunks)),
            dma((hs - 1, hop_chunks)),
            dma((hs - 1, hop_chunks)),
            dma((hs - 1, hop_chunks)),
            dma((hs,)),
            dma((hs,)),
            dma((hs - 1,)),
            dma((hs - 1,)),
        ],
        compiler_params=pltpu.CompilerParams(
            collective_id=0, has_side_effects=True, vmem_limit_bytes=60 << 20
        ),
        name="matern_product",
    )(src_codes, src_exps.T, signs, tgt_codes, tgt_exps.T)
    return out.T


def solution(mesh):
    placed = (
        P(("grp", "blk"), None),
        P(("grp", "blk"), None),
        P(("grp", "blk"), None),
        P("blk", None),
        P("blk", None),
    )
    return jax.shard_map(
        per_device, mesh=mesh, in_specs=placed, out_specs=P("blk", "grp"), check_vma=False
    )
```

```python
import functools
import math

import jax
import jax.numpy as jnp
from jax import lax
from jax.experimental import pallas as pl
from jax.experimental.pallas import tpu as pltpu
from jax.sharding import PartitionSpec as P

kernel_rate = 20.0
lanes = 128
src_chunks = 4
hop_chunks = 2
slab = 512
smallest = 2.0**-40
MESH = pl.DeviceIdType.MESH


def row_slice(start, size):
    return pl.ds(pl.multiple_of(start, size), size)


def dequantize_rows(codes, exps, start, count, gain, dst):
    levels = exps[:, row_slice(start, count)]
    factor = jnp.where(
        levels == 0,
        gain * 2.0**-9,
        jnp.where(levels == 1, gain * 2.0**-8, jnp.where(levels == 2, gain * 2.0**-7, gain * 2.0**-6)),
    ).astype(jnp.float32)
    factor = jnp.transpose(factor)
    blocks = exps.shape[0]
    width = codes.shape[1] // blocks
    total = None
    for j in range(blocks):
        columns = slice(j * width, (j + 1) * width)
        points = codes[row_slice(start, count), columns].astype(jnp.float32) * factor[:, j : j + 1]
        dst[row_slice(start, count), columns] = points.astype(jnp.bfloat16)
        total = points * points if total is None else total + points * points
    return total


def square_rows(points_ref, start, count):
    total = None
    for j in range(points_ref.shape[1] // lanes):
        points = points_ref[row_slice(start, count), j * lanes : (j + 1) * lanes].astype(jnp.float32)
        total = points * points if total is None else total + points * points
    return total


def kernel(
    ng, nb, sc_hbm, se_hbm, sg_hbm, tc_hbm, te_hbm, out_ref,
    sc, se, sg, tc, te, src, ssq, tgt, tsq, rhs, mat, acc,
    plane_send, plane_recv, hop_send, hop_recv, total,
    load_sem, core_send_sem, core_recv_sem, x_send_sem, x_recv_sem, f_send_sem, f_recv_sem,
    p_send_sem, p_recv_sem, h_send_sem, h_recv_sem,
):
    g = lax.axis_index("grp")
    b = lax.axis_index("blk")
    hs = nb // 2
    h, c = b // 2, lax.rem(b, 2)
    rows, width = sc.shape
    trows = tc.shape[0]
    rhs_count = sg.shape[1]
    part = rhs_count // ng
    half = trows // 2
    chunk = half // hop_chunks
    src_chunk = rows // src_chunks

    partner = (g, b + 1 - 2 * c)
    peers = [(g, lax.rem(h + j, hs) * 2 + c) for j in range(1, hs)]
    owners = [(g, lax.rem(h - j + hs, hs) * 2 + c) for j in range(1, hs)]
    plane = [(lax.rem(g + i, ng), b) for i in range(1, ng)]
    low, high = lax.rem(g, 2), lax.rem(g // 2, 2)
    side = lax.rem(low + high, 2)
    forward_to = [(g + 1 - 2 * low, b), (g + 2 - 4 * high, b)]

    load_te = pltpu.make_async_copy(te_hbm, te, load_sem.at[0])
    load_te.start()
    load_tc = pltpu.make_async_copy(tc_hbm, tc, load_sem.at[1])
    load_tc.start()
    load_se = pltpu.make_async_copy(se_hbm, se, load_sem.at[2])
    load_se.start()
    load_sc = []
    for k in range(src_chunks):
        piece = pl.ds(k * src_chunk, src_chunk)
        load_sc.append(pltpu.make_async_copy(sc_hbm.at[piece], sc.at[piece], load_sem.at[4 + k]))
        load_sc[-1].start()
    load_sg = pltpu.make_async_copy(sg_hbm, sg, load_sem.at[3])
    load_sg.start()

    barrier = pltpu.get_barrier_semaphore()
    greeted = [partner] + peers + plane
    for device in greeted:
        pl.semaphore_signal(barrier, inc=1, device_id=device, device_id_type=MESH)

    def own_targets(part_index):
        start = part_index * half
        squares = dequantize_rows(tc, te, start, half, -2.0, tgt.at[0])
        tsq[0, pl.ds(part_index, 1), :] = 0.25 * jnp.sum(jnp.transpose(squares), axis=0, keepdims=True)

    load_te.wait()
    load_tc.wait()
    own_targets(side)
    pl.semaphore_wait(barrier, len(greeted))

    def hop_rows(which, q):
        return row_slice(which * half + q * chunk, chunk)

    def x_copy(j, q):
        piece = hop_rows(side, q)
        return pltpu.make_async_remote_copy(
            src_ref=tgt.at[0, piece], dst_ref=tgt.at[j, piece],
            send_sem=x_send_sem.at[j - 1, q], recv_sem=x_recv_sem.at[j - 1, q],
            device_id=peers[j - 1], device_id_type=MESH,
        )

    def f_copy(j, q, which):
        piece = hop_rows(which, q)
        return pltpu.make_async_remote_copy(
            src_ref=tgt.at[j, piece], dst_ref=tgt.at[j, piece],
            send_sem=f_send_sem.at[j - 1, q], recv_sem=f_recv_sem.at[j - 1, q],
            device_id=forward_to[q % 2], device_id_type=MESH,
        )

    for q in range(hop_chunks):
        for j in range(1, hs):
            x_copy(j, q).start()
    own_targets(1 - side)

    def forward(q):
        for j in range(1, hs):
            x_copy(j, q).wait_recv()
            f_copy(j, q, side).start()

    def src_copy(k):
        return pltpu.make_async_remote_copy(
            src_ref=src.at[0, pl.ds(k * src_chunk, src_chunk)],
            dst_ref=src.at[1, pl.ds(k * src_chunk, src_chunk)],
            send_sem=core_send_sem.at[k], recv_sem=core_recv_sem.at[k],
            device_id=partner, device_id_type=MESH,
        )

    rhs_copy = pltpu.make_async_remote_copy(
        src_ref=rhs.at[0], dst_ref=rhs.at[1],
        send_sem=core_send_sem.at[src_chunks], recv_sem=core_recv_sem.at[src_chunks],
        device_id=partner, device_id_type=MESH,
    )

    def keep_source_squares(slot, start, squares):
        summed = jnp.sum(squares, axis=1, keepdims=True)
        ssq[slot, row_slice(start, lanes), :] = jnp.broadcast_to(summed, (lanes, lanes))

    load_se.wait()
    for k in range(src_chunks):
        load_sc[k].wait()

        @pl.loop(0, src_chunk // lanes)
        def _(i):
            start = k * src_chunk + i * lanes
            keep_source_squares(0, start, dequantize_rows(sc, se, start, lanes, 1.0, src.at[0]))

        src_copy(k).start()

    load_sg.wait()

    @pl.loop(0, rows // lanes)
    def _(i):
        signs = sg[row_slice(i * lanes, lanes), :].astype(jnp.float32)
        values = jnp.transpose(2.0 * signs - 1.0)
        rhs[0, :, row_slice(i * lanes, lanes)] = values.astype(jnp.bfloat16)

    rhs_copy.start()
    forward(0)

    rate = kernel_rate / math.sqrt(width)

    def matern_slabs(slot, j):
        target_sq = jnp.concatenate([tsq[j, 0:1, :], tsq[j, 1:2, :]], axis=1)

        @pl.loop(0, rows // slab)
        def _(i):
            piece = row_slice(i * slab, slab)
            inner = lax.dot_general(
                src[slot, piece, :], tgt[j], (((1,), (1,)), ((), ())),
                preferred_element_type=jnp.float32,
            )
            source_sq = ssq[slot, piece, :]
            source_sq = jnp.concatenate([source_sq] * (trows // lanes), axis=1)
            squared = jnp.maximum((source_sq + target_sq) + inner, smallest)
            distance = squared * lax.rsqrt(squared)
            decay = jnp.exp2(distance * (-rate * math.log2(math.e)))
            growth = 1.0 + distance * (rate + distance * (rate * rate / 3.0))
            mat[slot, piece, :] = (growth * decay).astype(jnp.bfloat16)

    def plane_copies(j):
        copies = []
        for i in range(1, ng):
            copies.append(pltpu.make_async_remote_copy(
                src_ref=plane_send.at[j, row_slice(plane[i - 1][0] * part, part)],
                dst_ref=plane_recv.at[j, i - 1],
                send_sem=p_send_sem.at[j], recv_sem=p_recv_sem.at[j],
                device_id=plane[i - 1], device_id_type=MESH,
            ))
        return copies

    def multiply_and_send(j):
        sums = jnp.dot(rhs[0], mat[0], preferred_element_type=jnp.float32)
        sums = sums + jnp.dot(rhs[1], mat[1], preferred_element_type=jnp.float32)
        acc[...] = sums
        plane_send[j] = sums.astype(jnp.bfloat16)
        for copy in plane_copies(j):
            copy.start()
        total[j] = acc[row_slice(g * part, part), :]

    def plane_total(j):
        pltpu.make_async_copy(plane_recv.at[j], plane_recv.at[j], p_recv_sem.at[j]).wait()
        sums = total[j]
        for i in range(ng - 1):
            sums = sums + plane_recv[j, i].astype(jnp.float32)
        return sums

    matern_slabs(0, 0)
    forward(1)
    for k in range(src_chunks):
        src_copy(k).wait_recv()

    @pl.loop(0, rows // lanes)
    def _(i):
        keep_source_squares(1, i * lanes, square_rows(src.at[1], i * lanes, lanes))

    matern_slabs(1, 0)
    rhs_copy.wait_recv()
    multiply_and_send(0)
    for q in range(2, hop_chunks):
        forward(q)

    def hop_copy(j):
        return pltpu.make_async_remote_copy(
            src_ref=hop_send.at[j - 1], dst_ref=hop_recv.at[j - 1],
            send_sem=h_send_sem.at[j - 1], recv_sem=h_recv_sem.at[j - 1],
            device_id=owners[j - 1], device_id_type=MESH,
        )

    def target_squares(j, which):
        squares = square_rows(tgt.at[j], which * half, half)
        tsq[j, pl.ds(which, 1), :] = 0.25 * jnp.sum(jnp.transpose(squares), axis=0, keepdims=True)

    for j in range(1, hs):
        target_squares(j, side)
        for q in range(hop_chunks):
            f_copy(j, q, 1 - side).wait_recv()
        target_squares(j, 1 - side)
        matern_slabs(0, j)
        matern_slabs(1, j)
        multiply_and_send(j)

    result = plane_total(0)
    for j in range(1, hs):
        hop_send[j - 1] = plane_total(j)
        hop_copy(j).start()
    for j in range(1, hs):
        hop_copy(j).wait_recv()
        result = result + hop_recv[j - 1]
    out_ref[...] = result * (4.0 / math.sqrt(rows * ng * nb))

    for j in range(1, hs):
        for q in range(hop_chunks):
            x_copy(j, q).wait_send()
            f_copy(j, q, side).wait_send()
        hop_copy(j).wait_send()
    for k in range(src_chunks):
        src_copy(k).wait_send()
    rhs_copy.wait_send()
    for j in range(hs):
        pltpu.make_async_copy(plane_recv.at[j], plane_recv.at[j], p_send_sem.at[j]).wait()


def per_device(src_codes, src_exps, signs, tgt_codes, tgt_exps):
    ng, nb = lax.axis_size("grp"), lax.axis_size("blk")
    hs = nb // 2
    rows, width = src_codes.shape
    trows = tgt_codes.shape[0]
    rhs_count = signs.shape[1]
    blocks = src_exps.shape[1]
    part = rhs_count // ng
    f32, bf16, i32 = jnp.float32, jnp.bfloat16, jnp.int32
    dma = pltpu.SemaphoreType.DMA
    out = pl.pallas_call(
        functools.partial(kernel, ng, nb),
        out_shape=jax.ShapeDtypeStruct((part, trows), f32),
        in_specs=[pl.BlockSpec(memory_space=pl.ANY)] * 5,
        out_specs=pl.BlockSpec(memory_space=pltpu.VMEM),
        scratch_shapes=[
            pltpu.VMEM((rows, width), i32),
            pltpu.VMEM((blocks, rows), i32),
            pltpu.VMEM((rows, rhs_count), i32),
            pltpu.VMEM((trows, width), i32),
            pltpu.VMEM((blocks, trows), i32),
            pltpu.VMEM((2, rows, width), bf16),
            pltpu.VMEM((2, rows, lanes), f32),
            pltpu.VMEM((hs, trows, width), bf16),
            pltpu.VMEM((hs, 2, trows // 2), f32),
            pltpu.VMEM((2, rhs_count, rows), bf16),
            pltpu.VMEM((2, rows, trows), bf16),
            pltpu.VMEM((rhs_count, trows), f32),
            pltpu.VMEM((hs, rhs_count, trows), bf16),
            pltpu.VMEM((hs, ng - 1, part, trows), bf16),
            pltpu.VMEM((hs - 1, part, trows), f32),
            pltpu.VMEM((hs - 1, part, trows), f32),
            pltpu.VMEM((hs, part, trows), f32),
            dma((4 + src_chunks,)),
            dma((src_chunks + 1,)),
            dma((src_chunks + 1,)),
            dma((hs - 1, hop_chunks)),
            dma((hs - 1, hop_chunks)),
            dma((hs - 1, hop_chunks)),
            dma((hs - 1, hop_chunks)),
            dma((hs,)),
            dma((hs,)),
            dma((hs - 1,)),
            dma((hs - 1,)),
        ],
        compiler_params=pltpu.CompilerParams(
            collective_id=0, has_side_effects=True, vmem_limit_bytes=60 << 20
        ),
        name="matern_product",
    )(src_codes, src_exps.T, signs, tgt_codes, tgt_exps.T)
    return out.T


def solution(mesh):
    placed = (
        P(("grp", "blk"), None),
        P(("grp", "blk"), None),
        P(("grp", "blk"), None),
        P("blk", None),
        P("blk", None),
    )
    return jax.shard_map(
        per_device, mesh=mesh, in_specs=placed, out_specs=P("blk", "grp"), check_vma=False
    )
```

```python
import functools
import math

import jax
import jax.numpy as jnp
from jax import lax
from jax.experimental import pallas as pl
from jax.experimental.pallas import tpu as pltpu
from jax.sharding import PartitionSpec as P

kernel_rate = 20.0
lanes = 128
src_chunks = 4
hop_chunks = 2
slab = 512
smallest = 2.0**-40
MESH = pl.DeviceIdType.MESH


def row_slice(start, size):
    return pl.ds(pl.multiple_of(start, size), size)


def dequantize_rows(codes, exps, start, count, gain, dst):
    levels = exps[:, row_slice(start, count)]
    factor = jnp.where(
        levels == 0,
        gain * 2.0**-9,
        jnp.where(levels == 1, gain * 2.0**-8, jnp.where(levels == 2, gain * 2.0**-7, gain * 2.0**-6)),
    ).astype(jnp.float32)
    factor = jnp.transpose(factor)
    blocks = exps.shape[0]
    width = codes.shape[1] // blocks
    total = None
    for j in range(blocks):
        columns = slice(j * width, (j + 1) * width)
        points = codes[row_slice(start, count), columns].astype(jnp.float32) * factor[:, j : j + 1]
        dst[row_slice(start, count), columns] = points.astype(jnp.bfloat16)
        total = points * points if total is None else total + points * points
    return total


def square_rows(points_ref, start, count):
    total = None
    for j in range(points_ref.shape[1] // lanes):
        points = points_ref[row_slice(start, count), j * lanes : (j + 1) * lanes].astype(jnp.float32)
        total = points * points if total is None else total + points * points
    return total


def kernel(
    ng, nb, sc_hbm, se_hbm, sg_hbm, tc_hbm, te_hbm, out_ref,
    sc, se, sg, tc, te, src, ssq, tgt, tsq, rhs, mat, acc,
    sum_send, sum_recv, total,
    load_sem, core_send_sem, core_recv_sem, x_send_sem, x_recv_sem, f_send_sem, f_recv_sem,
    s_send_sem, s_recv_sem,
):
    g = lax.axis_index("grp")
    b = lax.axis_index("blk")
    hs = nb // 2
    h, c = b // 2, lax.rem(b, 2)
    rows, width = sc.shape
    trows = tc.shape[0]
    rhs_count = sg.shape[1]
    part = rhs_count // ng
    half = trows // 2
    chunk = half // hop_chunks
    src_chunk = rows // src_chunks

    partner = (g, b + 1 - 2 * c)
    peers = [(g, lax.rem(h + j, hs) * 2 + c) for j in range(1, hs)]
    takers = [
        [(lax.rem(g + i, ng), lax.rem(h - j + hs, hs) * 2 + c) for i in range(1 if j == 0 else 0, ng)]
        for j in range(hs)
    ]
    low, high = lax.rem(g, 2), lax.rem(g // 2, 2)
    side = lax.rem(low + high, 2)
    forward_to = [(g + 1 - 2 * low, b), (g + 2 - 4 * high, b)]

    load_te = pltpu.make_async_copy(te_hbm, te, load_sem.at[0])
    load_te.start()
    load_tc = pltpu.make_async_copy(tc_hbm, tc, load_sem.at[1])
    load_tc.start()
    load_se = pltpu.make_async_copy(se_hbm, se, load_sem.at[2])
    load_se.start()
    load_sc = []
    for k in range(src_chunks):
        piece = pl.ds(k * src_chunk, src_chunk)
        load_sc.append(pltpu.make_async_copy(sc_hbm.at[piece], sc.at[piece], load_sem.at[4 + k]))
        load_sc[-1].start()
    load_sg = pltpu.make_async_copy(sg_hbm, sg, load_sem.at[3])
    load_sg.start()

    barrier = pltpu.get_barrier_semaphore()
    greeted = [partner] + [device for group in takers for device in group]
    for device in greeted:
        pl.semaphore_signal(barrier, inc=1, device_id=device, device_id_type=MESH)

    def own_targets(part_index):
        start = part_index * half
        squares = dequantize_rows(tc, te, start, half, -2.0, tgt.at[0])
        tsq[0, pl.ds(part_index, 1), :] = 0.25 * jnp.sum(jnp.transpose(squares), axis=0, keepdims=True)

    load_te.wait()
    load_tc.wait()
    own_targets(side)
    pl.semaphore_wait(barrier, len(greeted))

    def hop_rows(which, q):
        return row_slice(which * half + q * chunk, chunk)

    def x_copy(j, q):
        piece = hop_rows(side, q)
        return pltpu.make_async_remote_copy(
            src_ref=tgt.at[0, piece], dst_ref=tgt.at[j, piece],
            send_sem=x_send_sem.at[j - 1, q], recv_sem=x_recv_sem.at[j - 1, q],
            device_id=peers[j - 1], device_id_type=MESH,
        )

    def f_copy(j, q, which):
        piece = hop_rows(which, q)
        return pltpu.make_async_remote_copy(
            src_ref=tgt.at[j, piece], dst_ref=tgt.at[j, piece],
            send_sem=f_send_sem.at[j - 1, q], recv_sem=f_recv_sem.at[j - 1, q],
            device_id=forward_to[q % 2], device_id_type=MESH,
        )

    for q in range(hop_chunks):
        for j in range(1, hs):
            x_copy(j, q).start()
    own_targets(1 - side)

    def forward(q):
        for j in range(1, hs):
            x_copy(j, q).wait_recv()
            f_copy(j, q, side).start()

    def src_copy(k):
        return pltpu.make_async_remote_copy(
            src_ref=src.at[0, pl.ds(k * src_chunk, src_chunk)],
            dst_ref=src.at[1, pl.ds(k * src_chunk, src_chunk)],
            send_sem=core_send_sem.at[k], recv_sem=core_recv_sem.at[k],
            device_id=partner, device_id_type=MESH,
        )

    rhs_copy = pltpu.make_async_remote_copy(
        src_ref=rhs.at[0], dst_ref=rhs.at[1],
        send_sem=core_send_sem.at[src_chunks], recv_sem=core_recv_sem.at[src_chunks],
        device_id=partner, device_id_type=MESH,
    )

    def keep_source_squares(slot, start, squares):
        summed = jnp.sum(squares, axis=1, keepdims=True)
        ssq[slot, row_slice(start, lanes), :] = jnp.broadcast_to(summed, (lanes, lanes))

    load_se.wait()
    for k in range(src_chunks):
        load_sc[k].wait()

        @pl.loop(0, src_chunk // lanes)
        def _(i):
            start = k * src_chunk + i * lanes
            keep_source_squares(0, start, dequantize_rows(sc, se, start, lanes, 1.0, src.at[0]))

        src_copy(k).start()

    load_sg.wait()

    @pl.loop(0, rows // lanes)
    def _(i):
        signs = sg[row_slice(i * lanes, lanes), :].astype(jnp.float32)
        values = jnp.transpose(2.0 * signs - 1.0)
        rhs[0, :, row_slice(i * lanes, lanes)] = values.astype(jnp.bfloat16)

    rhs_copy.start()
    forward(0)

    rate = kernel_rate / math.sqrt(width)

    def matern_slabs(slot, j):
        target_sq = jnp.concatenate([tsq[j, 0:1, :], tsq[j, 1:2, :]], axis=1)

        @pl.loop(0, rows // slab)
        def _(i):
            piece = row_slice(i * slab, slab)
            inner = lax.dot_general(
                src[slot, piece, :], tgt[j], (((1,), (1,)), ((), ())),
                preferred_element_type=jnp.float32,
            )
            source_sq = ssq[slot, piece, :]
            source_sq = jnp.concatenate([source_sq] * (trows // lanes), axis=1)
            squared = jnp.maximum((source_sq + target_sq) + inner, smallest)
            distance = squared * lax.rsqrt(squared)
            decay = jnp.exp2(distance * (-rate * math.log2(math.e)))
            growth = 1.0 + distance * (rate + distance * (rate * rate / 3.0))
            mat[slot, piece, :] = (growth * decay).astype(jnp.bfloat16)

    def sum_copies(j):
        copies = []
        for i, taker in enumerate(takers[j]):
            copies.append(pltpu.make_async_remote_copy(
                src_ref=sum_send.at[j, row_slice(taker[0] * part, part)],
                dst_ref=sum_recv.at[j, i],
                send_sem=s_send_sem.at[j], recv_sem=s_recv_sem.at[j],
                device_id=taker, device_id_type=MESH,
            ))
        return copies

    def multiply_and_send(j):
        sums = jnp.dot(rhs[0], mat[0], preferred_element_type=jnp.float32)
        sums = sums + jnp.dot(rhs[1], mat[1], preferred_element_type=jnp.float32)
        sum_send[j] = sums.astype(jnp.bfloat16)
        for copy in sum_copies(j):
            copy.start()
        if j == 0:
            acc[...] = sums
            total[...] = acc[row_slice(g * part, part), :]

    def sums_bytes(j, sem):
        count = len(takers[j])
        arrived = sum_recv.at[j, pl.ds(0, count)]
        return pltpu.make_async_copy(arrived, arrived, sem.at[j])

    matern_slabs(0, 0)
    forward(1)
    for k in range(src_chunks):
        src_copy(k).wait_recv()

    @pl.loop(0, rows // lanes)
    def _(i):
        keep_source_squares(1, i * lanes, square_rows(src.at[1], i * lanes, lanes))

    matern_slabs(1, 0)
    rhs_copy.wait_recv()
    multiply_and_send(0)
    for q in range(2, hop_chunks):
        forward(q)

    def target_squares(j, which):
        squares = square_rows(tgt.at[j], which * half, half)
        tsq[j, pl.ds(which, 1), :] = 0.25 * jnp.sum(jnp.transpose(squares), axis=0, keepdims=True)

    for j in range(1, hs):
        target_squares(j, side)
        for q in range(hop_chunks):
            f_copy(j, q, 1 - side).wait_recv()
        target_squares(j, 1 - side)
        matern_slabs(0, j)
        matern_slabs(1, j)
        multiply_and_send(j)

    result = total[...]
    for j in range(hs):
        sums_bytes(j, s_recv_sem).wait()
        for i in range(len(takers[j])):
            result = result + sum_recv[j, i].astype(jnp.float32)
    out_ref[...] = result * (4.0 / math.sqrt(rows * ng * nb))

    for j in range(1, hs):
        for q in range(hop_chunks):
            x_copy(j, q).wait_send()
            f_copy(j, q, side).wait_send()
    for k in range(src_chunks):
        src_copy(k).wait_send()
    rhs_copy.wait_send()
    for j in range(hs):
        sums_bytes(j, s_send_sem).wait()


def per_device(src_codes, src_exps, signs, tgt_codes, tgt_exps):
    ng, nb = lax.axis_size("grp"), lax.axis_size("blk")
    hs = nb // 2
    rows, width = src_codes.shape
    trows = tgt_codes.shape[0]
    rhs_count = signs.shape[1]
    blocks = src_exps.shape[1]
    part = rhs_count // ng
    f32, bf16, i32 = jnp.float32, jnp.bfloat16, jnp.int32
    dma = pltpu.SemaphoreType.DMA
    out = pl.pallas_call(
        functools.partial(kernel, ng, nb),
        out_shape=jax.ShapeDtypeStruct((part, trows), f32),
        in_specs=[pl.BlockSpec(memory_space=pl.ANY)] * 5,
        out_specs=pl.BlockSpec(memory_space=pltpu.VMEM),
        scratch_shapes=[
            pltpu.VMEM((rows, width), i32),
            pltpu.VMEM((blocks, rows), i32),
            pltpu.VMEM((rows, rhs_count), i32),
            pltpu.VMEM((trows, width), i32),
            pltpu.VMEM((blocks, trows), i32),
            pltpu.VMEM((2, rows, width), bf16),
            pltpu.VMEM((2, rows, lanes), f32),
            pltpu.VMEM((hs, trows, width), bf16),
            pltpu.VMEM((hs, 2, trows // 2), f32),
            pltpu.VMEM((2, rhs_count, rows), bf16),
            pltpu.VMEM((2, rows, trows), bf16),
            pltpu.VMEM((rhs_count, trows), f32),
            pltpu.VMEM((hs, rhs_count, trows), bf16),
            pltpu.VMEM((hs, ng, part, trows), bf16),
            pltpu.VMEM((part, trows), f32),
            dma((4 + src_chunks,)),
            dma((src_chunks + 1,)),
            dma((src_chunks + 1,)),
            dma((hs - 1, hop_chunks)),
            dma((hs - 1, hop_chunks)),
            dma((hs - 1, hop_chunks)),
            dma((hs - 1, hop_chunks)),
            dma((hs,)),
            dma((hs,)),
        ],
        compiler_params=pltpu.CompilerParams(
            collective_id=0, has_side_effects=True, vmem_limit_bytes=60 << 20
        ),
        name="matern_product",
    )(src_codes, src_exps.T, signs, tgt_codes, tgt_exps.T)
    return out.T


def solution(mesh):
    placed = (
        P(("grp", "blk"), None),
        P(("grp", "blk"), None),
        P(("grp", "blk"), None),
        P("blk", None),
        P("blk", None),
    )
    return jax.shard_map(
        per_device, mesh=mesh, in_specs=placed, out_specs=P("blk", "grp"), check_vma=False
    )
```
